1024 devices in a mesh: dp: 64 (over y, z_hi, core), tensor: 16 (over z_lo, x).
Axes of the slice: x: 8, y: 8, z: 8 (z_hi: 4, z_lo: 2; z = z_hi * 2 + z_lo), core: 2. Of those that a mesh axis runs over, the one named last changes fastest.
Arguments:
- tokens: bfloat16 [131072, 3072], P('dp', 'tensor'), may hold values from -6 to 6
- cotangent: bfloat16 [131072, 1024], P('dp'), may hold values from -8 to 8
- weight: bfloat16 [3072, 1024], P('tensor'), may hold values from -6 to 6
- momentum: bfloat16 [64, 3072, 1024], P('dp', 'tensor'), may hold values from -3.5 to 3.5
- threshold: int32 [1024], replicated, may hold values from 2 to 8
Outputs:
- key_values: bfloat16 [131072, 1024], P(('dp', 'tensor'))
- input_grad: bfloat16 [131072, 3072], P('dp', 'tensor')
- new_momentum: bfloat16 [64, 3072, 1024], P('dp', 'tensor')
- new_weight: bfloat16 [3072, 1024], P('tensor', 'dp')
The draws below stay inside these ranges and needn't reach their ends.
All inputs are finite; a program needn't handle non-finite values.
Results may differ from the reference program's by a relative error of at most 0.017.
Values may be sent and summed in bfloat16 or wider, within the bound.
A program may use at most 32 MiB of HBM per device.

```python
import jax
import jax.numpy as jnp
from jax import lax

D = 3072
KVW = 1024
GROUP_ROWS = 2048
TOKENS = 131072
N_DP = 64
N_TENSOR = 16


def place_ends(drawn, key, smallest, largest):
    spot = [jax.random.randint(jax.random.fold_in(key, axis), (), 0, length) for axis, length in enumerate(drawn.shape)]
    longest = drawn.shape.index(max(drawn.shape))
    neighbour = spot[:longest] + [(spot[longest] + 1) % drawn.shape[longest]] + spot[longest + 1:]
    return drawn.at[tuple(spot)].set(smallest).at[tuple(neighbour)].set(largest)


def strengthened(entries, key, source, target, blocks, factor):
    def block_of(dim):
        return (jnp.arange(entries.shape[dim]) // (entries.shape[dim] // blocks)).reshape((-1,) + (1,) * (entries.ndim - 1 - dim))

    near = jax.random.permutation(key, blocks)[block_of(target)]
    far = (block_of(target) + blocks // 2) % blocks
    return jnp.where((block_of(source) == near) | (block_of(source) == far), factor * entries, entries)


def shard_levels(key, shape, pieces, least, top_value):
    gain = 1.0
    for position, parts in pieces:
        heights = jax.random.uniform(jax.random.fold_in(jax.random.fold_in(key, 6), position), (parts,), jnp.float32, least / len(pieces), top_value / len(pieces))
        gain = gain * jnp.repeat(jnp.exp(heights), shape[position] // parts).reshape((-1,) + (1,) * (len(shape) - 1 - position))
    return gain


def bell_draw(rng, extent, scale, most, shards=(), dtype=jnp.bfloat16):
    result = jax.random.normal(rng, extent, jnp.float32) * scale
    if len(shards) > 0:
        result = shard_levels(rng, extent, shards, -0.22, 0.18) * result
    return jnp.clip(result, min=-most, max=most).astype(dtype)


def gaussian_with(key, dims, width, reach, shards, heavy, dtype=jnp.bfloat16):
    array = width * jax.random.normal(key, dims, jnp.float32)
    if shards:
        array = array * shard_levels(key, dims, shards, -0.22, 0.18)
    return jnp.clip(strengthened(array, jax.random.fold_in(key, 3), *heavy), -reach, reach).astype(dtype)


def setup_inputs(seed: int = 0) -> dict:
    key_list = jax.random.split(jax.random.key(seed), 6)
    tokens = bell_draw(key_list[0], (TOKENS, D), 1.0, 6.0, ((0, 64), (1, 16)))
    cotangent = bell_draw(key_list[1], (TOKENS, KVW), 1.0, 8.0, ((0, 64),))
    weight = bell_draw(key_list[2], (D, KVW), 1.0, 6.0, ((0, 16),))
    momentum = gaussian_with(key_list[3], (N_DP, D, KVW), 0.2, 3.5, ((0, 64), (1, 16)), (0, 2, 64, 4.0))
    threshold = place_ends(jax.random.randint(key_list[4], (KVW,), 2, 9), jax.random.fold_in(key_list[4], 1), 2, 8).astype(jnp.int32)
    return {"tokens": tokens, "cotangent": cotangent, "weight": weight, "momentum": momentum, "threshold": threshold}


def reference(tokens, cotangent, weight, momentum, threshold):
    inverse = D ** -0.5
    feature_share = D // N_TENSOR
    token_blocks = tokens.reshape(TOKENS, N_TENSOR, feature_share).transpose(1, 0, 2)
    weight_blocks = weight.reshape(N_TENSOR, feature_share, KVW)

    def add_partial(running, pair):
        token_block, weight_block = pair
        partial_value = jnp.dot(token_block, weight_block, preferred_element_type=jnp.float32) * inverse
        return running + partial_value.astype(jnp.bfloat16).astype(jnp.float32), None

    key_total, unused = lax.scan(add_partial, jnp.zeros((TOKENS, KVW), jnp.float32), (token_blocks, weight_blocks))
    key_values = key_total.astype(jnp.bfloat16)
    input_grad = (lax.dot_general(cotangent, weight, (((1,), (1,)), ((), ())), preferred_element_type=jnp.float32) * inverse).astype(jnp.bfloat16)
    token_groups = tokens.reshape(N_DP, GROUP_ROWS, D)
    cot_groups = cotangent.reshape(N_DP, GROUP_ROWS, KVW)

    def replica_step(votes, triple):
        group_tokens, group_cot, old_moment = triple
        gradient = lax.dot_general(group_tokens, group_cot, (((0,), (0,)), ((), ())), preferred_element_type=jnp.float32) * inverse
        fresh = (0.9 * old_moment.astype(jnp.float32) + 0.1 * gradient).astype(jnp.bfloat16)
        votes = votes + jnp.clip(fresh.astype(jnp.float32) / 0.125, -1.0, 1.0)
        return votes, fresh

    votes, new_momentum = lax.scan(replica_step, jnp.zeros((D, KVW), jnp.float32), (token_groups, cot_groups, momentum))
    update = jnp.clip(votes / threshold.astype(jnp.float32)[None, :], -1.0, 1.0)
    new_weight = (weight.astype(jnp.float32) - 0.5 * update).astype(jnp.bfloat16)
    return key_values, input_grad, new_momentum, new_weight
```

```python
import jax
import jax.numpy as jnp
from jax import lax
from jax.experimental import pallas as pl
from jax.experimental.pallas import tpu as pltpu
from jax.sharding import PartitionSpec as P

D = 3072
INVERSE = D ** (-0.5)
MESH = pl.DeviceIdType.MESH
F32 = jnp.float32
BF16 = jnp.bfloat16

NX, NY, NZ = 8, 8, 4
FEAT, ROWS, COLS = 192, 2048, 1024
HALF = COLS // 2
AHEAD = (4, 3, 5, 2, 6, 1, 7, 0)
SLOT = {d: s for s, d in enumerate(AHEAD)}


def place():
    dp, tensor = lax.axis_index("dp"), lax.axis_index("tensor")
    return dp // 8, (dp // 2) % 4, dp % 2, tensor // 8, tensor % 8


def device(y, z_hi, core, z_lo, x):
    return (y * 8 + z_hi * 2 + core, z_lo * 8 + x)


def remote(src, dst, sems, i, peer):
    send, recv = sems
    return pltpu.make_async_remote_copy(
        src_ref=src,
        dst_ref=dst,
        send_sem=send.at[i],
        recv_sem=recv.at[i],
        device_id=peer,
        device_id_type=MESH,
    )


def clipped(m):
    return jnp.clip(m.astype(F32) * 8.0, -1.0, 1.0)


def main_kernel(
    tok, cot, w, mom,
    kv, ig, fresh, votes,
    tf, tt, ww, cv, mv, fv, gv, own, ring_out, ring_in, kvv, yin, zout, zin, vv,
    local, wsend, wrecv, tsend, trecv, xsend, xrecv, ysend, yrecv, zsend, zrecv,
):
    y, zh, c, zl, x = place()
    right = device(y, zh, c, zl, (x + 1) % NX)
    left = device(y, zh, c, zl, (x + NX - 1) % NX)
    pair = device(y, zh, c, 1 - zl, x)
    outer = device(y, (zh + 3 - 2 * zl) % NZ, c, 1 - zl, x)
    y_peers = [device((y + d) % NY, zh, c, zl, x) for d in range(1, NY)]
    z_peers = [device(y, (zh + d) % NZ, c, zl, x) for d in range(1, NZ)]

    barrier = pltpu.get_barrier_semaphore()
    peers = [right, left, pair, outer] + y_peers + z_peers
    for p in peers:
        pl.semaphore_signal(barrier, inc=1, device_id=p, device_id_type=MESH)

    mine = pl.multiple_of(zl * 1024, 1024)
    theirs = pl.multiple_of((1 - zl) * 1024, 1024)
    loads = [
        pltpu.make_async_copy(tok.at[:, pl.ds(mine, 1024)], tt.at[pl.ds(0, FEAT)], local.at[0]),
        pltpu.make_async_copy(w, ww.at[pl.ds(0, FEAT)], local.at[1]),
        pltpu.make_async_copy(tok, tf, local.at[2]),
        pltpu.make_async_copy(mom, mv, local.at[3]),
        pltpu.make_async_copy(cot, cv, local.at[4]),
    ]
    for load in loads:
        load.start()

    pl.semaphore_wait(barrier, len(peers))

    def piece(d):
        return pl.multiple_of(((x + d) % NX) * 128, 128)

    token_copies = {}

    def send_tokens(d):
        token_copies[d] = remote(
            tok.at[:, pl.ds(pl.multiple_of(theirs + piece(d), 128), 128)],
            tt.at[pl.ds(FEAT, FEAT), pl.ds(piece(d), 128)],
            (tsend, trecv), SLOT[d], pair,
        )
        token_copies[d].start()

    weight_copies = [
        remote(w.at[:, pl.ds(h * HALF, HALF)], ww.at[pl.ds(FEAT, FEAT), pl.ds(h * HALF, HALF)],
               (wsend, wrecv), h, to)
        for h, to in enumerate((pair, outer))
    ]
    weight_copies[1].start()
    send_tokens(4)
    weight_copies[0].start()
    for d in AHEAD[1:]:
        send_tokens(d)

    loads[2].wait()
    loads[3].wait()
    loads[4].wait()

    def grad_step(i, _):
        at = pl.ds(pl.multiple_of(i * 256, 256), 256)
        grad = lax.dot_general(tf[...], cv[:, at], (((1,), (0,)), ((), ())), preferred_element_type=F32)
        fv[:, at] = (0.9 * mv[:, at].astype(F32) + 0.1 * (grad * INVERSE)).astype(BF16)
        return _

    lax.fori_loop(0, COLS // 256, grad_step, 0)
    y_copies = [
        remote(fv.at[:, pl.ds(pl.multiple_of(((y + d) % NY) * 128, 128), 128)], yin.at[d - 1],
               (ysend, yrecv), d - 1, y_peers[d - 1])
        for d in range(1, NY)
    ]
    for q in y_copies:
        q.start()
    stores = [pltpu.make_async_copy(fv, fresh, local.at[5])]
    stores[0].start()

    loads[0].wait()
    loads[1].wait()
    for q in weight_copies:
        q.wait_recv()

    def own_partial(d):
        token_copies[d].wait_recv()
        rows = tt[:, pl.ds(piece(d), 128)]
        for h in range(2):
            cols = pl.ds(h * HALF, HALF)
            own[SLOT[d], :, cols] = INVERSE * lax.dot_general(
                rows, ww[:, cols], (((0,), (0,)), ((), ())), preferred_element_type=F32
            )

    messages = {}

    def owner(way, k):
        ahead = 4 - (k + 1) // 2
        return ahead if way == 0 else (NX - ahead) % NX

    def half(way, k):
        return pl.ds(((k + way) % 2) * HALF, HALF)

    def send_sum(way, k):
        total = own[SLOT[owner(way, k)], :, half(way, k)]
        if k >= 2:
            messages[way, k - 2].wait_recv()
            total = total + ring_in[way * 7 + k - 2].astype(F32)
        ring_out[way * 7 + k] = total.astype(BF16)
        messages[way, k] = remote(ring_out.at[way * 7 + k], ring_in.at[way * 7 + k], (xsend, xrecv),
                                  way * 7 + k, right if way == 0 else left)
        messages[way, k].start()

    def input_grad_part(first, last):
        def step(i, _):
            at = pl.ds(pl.multiple_of(i * 256, 256), 256)
            gv[:, at] = (
                lax.dot_general(ww[pl.ds(0, FEAT)], cv[at, :], (((1,), (1,)), ((), ())),
                                preferred_element_type=F32) * INVERSE
            ).astype(BF16)
            return _

        lax.fori_loop(first, last, step, 0)

    own_partial(4)
    for way in range(2):
        send_sum(way, 0)
    own_partial(3)
    send_sum(0, 1)
    own_partial(5)
    send_sum(1, 1)
    input_grad_part(0, 4)
    for way in range(2):
        send_sum(way, 2)
    own_partial(2)
    own_partial(6)
    for way in range(2):
        send_sum(way, 3)
    input_grad_part(4, 8)
    stores.append(pltpu.make_async_copy(gv, ig, local.at[6]))
    stores[1].start()
    for way in range(2):
        send_sum(way, 4)
    own_partial(1)
    own_partial(7)
    for way in range(2):
        send_sum(way, 5)
    own_partial(0)
    for way in range(2):
        send_sum(way, 6)

    my_block = pl.ds(pl.multiple_of(y * 128, 128), 128)
    total = clipped(fv[:, my_block])
    for d in range(1, NY):
        y_copies[d - 1].wait_recv()
        total = total + clipped(yin[d - 1])
    zout[...] = total.T
    z_copies = [
        remote(zout.at[pl.ds(pl.multiple_of(((zh + d) % NZ) * 32, 32), 32)], zin.at[d - 1],
               (zsend, zrecv), d - 1, z_peers[d - 1])
        for d in range(1, NZ)
    ]
    for q in z_copies:
        q.start()

    for k in (5, 6):
        for way in range(2):
            messages[way, k].wait_recv()
    for h in range(2):
        cols = pl.ds(h * HALF, HALF)
        from_left, from_right = ring_in[6 - h], ring_in[7 + 5 + h]
        kvv[:, cols] = (own[SLOT[0], :, cols] + from_left.astype(F32) + from_right.astype(F32)).astype(BF16)
    stores.append(pltpu.make_async_copy(kvv, kv, local.at[7]))
    stores[2].start()

    part = zout[pl.ds(pl.multiple_of(zh * 32, 32), 32), :]
    for d in range(1, NZ):
        z_copies[d - 1].wait_recv()
        part = part + zin[d - 1]
    vv[...] = part
    stores.append(pltpu.make_async_copy(vv, votes, local.at[8]))
    stores[3].start()

    for q in weight_copies + [token_copies[d] for d in AHEAD] + y_copies + z_copies:
        q.wait_send()
    for way in range(2):
        for k in range(7):
            messages[way, k].wait_send()
    for q in stores:
        q.wait()


def last_kernel(votes, w, thr, out, wv, wt, tt, arrived, local, send, recv):
    y, zh, c, zl, x = place()
    other = device(y, zh, 1 - c, zl, x)
    barrier = pltpu.get_barrier_semaphore()
    pl.semaphore_signal(barrier, inc=1, device_id=other, device_id_type=MESH)
    block = pl.ds(pl.multiple_of(y * 128, 128), 128)
    load = pltpu.make_async_copy(w.at[:, block], wv, local.at[0])
    load.start()
    limits = jnp.broadcast_to(thr[pl.ds(y, 1), :].astype(F32), (8, 128))
    tt[...] = limits.T
    pl.semaphore_wait(barrier, 1)
    copy = remote(votes.at[pl.ds(pl.multiple_of((1 - c) * 16, 16), 16)], arrived, (send, recv), 0, other)
    copy.start()
    load.wait()
    wt[...] = wv[...].astype(F32).T
    mine = pl.ds(pl.multiple_of(zh * 32 + c * 16, 16), 16)
    own_w = wt[mine, :]
    own_limits = tt[mine, 0:1]
    copy.wait_recv()
    total = votes[pl.ds(pl.multiple_of(c * 16, 16), 16), :] + arrived[...]
    out[...] = (own_w - 0.5 * jnp.clip(total / own_limits, -1.0, 1.0)).astype(BF16)
    copy.wait_send()


ANY = pl.BlockSpec(memory_space=pl.ANY)
VMEM = pl.BlockSpec(memory_space=pltpu.VMEM)
DMA = pltpu.SemaphoreType.DMA


def per_device(tokens, cotangent, weight, momentum, threshold):
    shape = jax.ShapeDtypeStruct
    kv, ig, fresh, votes = pl.pallas_call(
        main_kernel,
        out_shape=(
            shape((128, COLS), BF16),
            shape((FEAT, ROWS), BF16),
            shape((FEAT, COLS), BF16),
            shape((32, FEAT), F32),
        ),
        in_specs=[ANY] * 4,
        out_specs=[ANY] * 4,
        scratch_shapes=[
            pltpu.VMEM((FEAT, ROWS), BF16),
            pltpu.VMEM((2 * FEAT, 1024), BF16),
            pltpu.VMEM((2 * FEAT, COLS), BF16),
            pltpu.VMEM((ROWS, COLS), BF16),
            pltpu.VMEM((FEAT, COLS), BF16),
            pltpu.VMEM((FEAT, COLS), BF16),
            pltpu.VMEM((FEAT, ROWS), BF16),
            pltpu.VMEM((NX, 128, COLS), F32),
            pltpu.VMEM((14, 128, HALF), BF16),
            pltpu.VMEM((14, 128, HALF), BF16),
            pltpu.VMEM((128, COLS), BF16),
            pltpu.VMEM((NY - 1, FEAT, 128), BF16),
            pltpu.VMEM((128, FEAT), F32),
            pltpu.VMEM((NZ - 1, 32, FEAT), F32),
            pltpu.VMEM((32, FEAT), F32),
            DMA((9,)),
            DMA((2,)), DMA((2,)),
            DMA((8,)), DMA((8,)),
            DMA((14,)), DMA((14,)),
            DMA((7,)), DMA((7,)),
            DMA((3,)), DMA((3,)),
        ],
        compiler_params=pltpu.CompilerParams(
            collective_id=0, has_side_effects=True, vmem_limit_bytes=48 * 2**20
        ),
        cost_estimate=pl.CostEstimate(flops=2_400_000_000, bytes_accessed=7_000_000, transcendentals=0),
        name="keys_and_votes",
    )(tokens.T, cotangent, weight, momentum[0])
    new_weight = pl.pallas_call(
        last_kernel,
        out_shape=shape((16, FEAT), BF16),
        in_specs=[VMEM, ANY, VMEM],
        out_specs=VMEM,
        scratch_shapes=[
            pltpu.VMEM((FEAT, 128), BF16),
            pltpu.VMEM((128, FEAT), F32),
            pltpu.VMEM((128, 8), F32),
            pltpu.VMEM((16, FEAT), F32),
            DMA((1,)),
            DMA((1,)), DMA((1,)),
        ],
        compiler_params=pltpu.CompilerParams(collective_id=1, has_side_effects=True),
        name="other_core",
    )(votes, weight, threshold.reshape(8, 128))
    return kv, ig.T, fresh[None], new_weight.T


def solution(mesh):
    return jax.shard_map(
        per_device,
        mesh=mesh,
        in_specs=(P("dp", "tensor"), P("dp", None), P("tensor", None), P("dp", "tensor", None), P()),
        out_specs=(P(("dp", "tensor"), None), P("dp", "tensor"), P("dp", "tensor", None), P("tensor", "dp")),
        check_vma=False,
    )
```

```python
import jax
import jax.numpy as jnp
from jax import lax
from jax.experimental import pallas as pl
from jax.experimental.pallas import tpu as pltpu
from jax.sharding import PartitionSpec as P

D = 3072
INVERSE = D ** (-0.5)
MESH = pl.DeviceIdType.MESH
F32 = jnp.float32
BF16 = jnp.bfloat16

NX, NY, NZ = 8, 8, 4
LEADER = 2
FEAT, ROWS, COLS = 192, 2048, 1024
HALF, QUARTER = COLS // 2, COLS // 4
AHEAD = (4, 3, 5, 2, 6, 1, 7, 0)
SLOT = {d: s for s, d in enumerate(AHEAD)}


def place():
    dp, tensor = lax.axis_index("dp"), lax.axis_index("tensor")
    return dp // 8, (dp // 2) % 4, dp % 2, tensor // 8, tensor % 8


def device(y, z_hi, core, z_lo, x):
    return (y * 8 + z_hi * 2 + core, z_lo * 8 + x)


def remote(src, dst, sems, i, peer):
    send, recv = sems
    return pltpu.make_async_remote_copy(
        src_ref=src,
        dst_ref=dst,
        send_sem=send.at[i],
        recv_sem=recv.at[i],
        device_id=peer,
        device_id_type=MESH,
    )


def signal(semaphore, peer):
    pl.semaphore_signal(semaphore, inc=1, device_id=peer, device_id_type=MESH)


def clipped(m):
    return jnp.clip(m.astype(F32) * 8.0, -1.0, 1.0)


def main_kernel(
    tok, cot, w, mom, thr,
    kv, ig, fresh, new_w,
    tf, tt, ww, cv, mv, fv, gv, own, ring_out, ring_in, kvv, yin, zout, zin, wt, lt, nv,
    local, wsend, wrecv, tsend, trecv, xsend, xrecv, ysend, yrecv, zsend, zrecv, inside, others, ready,
):
    y, zh, c, zl, x = place()
    right = device(y, zh, c, zl, (x + 1) % NX)
    left = device(y, zh, c, zl, (x + NX - 1) % NX)
    pair = device(y, zh, c, 1 - zl, x)
    outer = device(y, (zh + 3 - 2 * zl) % NZ, c, 1 - zl, x)
    y_peers = [device((y + d) % NY, zh, c, zl, x) for d in range(1, NY)]
    z_peers = [device(y, (zh + d // 2) % NZ, (c + d) % 2, zl, x) for d in range(1, 2 * NZ)]

    barrier = pltpu.get_barrier_semaphore()
    from_leader = (x + NX - LEADER) % NX
    leads = from_leader == 0
    peers = [right, left, pair, outer]
    far = y_peers + z_peers
    for p in peers:
        signal(barrier, p)

    @pl.when(leads)
    def _():
        for p in far:
            signal(barrier, p)

    mine = pl.multiple_of(zl * 1024, 1024)
    theirs = pl.multiple_of((1 - zl) * 1024, 1024)
    loads = [
        pltpu.make_async_copy(tok.at[:, pl.ds(mine, 1024)], tt.at[pl.ds(0, FEAT)], local.at[0]),
        pltpu.make_async_copy(w, ww.at[pl.ds(0, FEAT)], local.at[1]),
        pltpu.make_async_copy(tok, tf, local.at[2]),
        pltpu.make_async_copy(mom, mv, local.at[3]),
        pltpu.make_async_copy(cot, cv, local.at[4]),
    ]
    for load in loads:
        load.start()

    @pl.when(leads)
    def _():
        pl.semaphore_wait(barrier, len(peers) + len(far))

    @pl.when(jnp.logical_not(leads))
    def _():
        pl.semaphore_wait(barrier, len(peers))

    def piece(d):
        return pl.multiple_of(((x + d) % NX) * 128, 128)

    token_copies = {}

    def send_tokens(d):
        token_copies[d] = remote(
            tok.at[:, pl.ds(pl.multiple_of(theirs + piece(d), 128), 128)],
            tt.at[pl.ds(FEAT, FEAT), pl.ds(piece(d), 128)],
            (tsend, trecv), SLOT[d], pair,
        )
        token_copies[d].start()

    weight_copies = [
        remote(w.at[:, pl.ds(q * QUARTER, QUARTER)], ww.at[pl.ds(FEAT, FEAT), pl.ds(q * QUARTER, QUARTER)],
               (wsend, wrecv), q, pair if q < 2 else outer)
        for q in range(4)
    ]
    send_tokens(4)
    for q in (2, 0, 3, 1):
        weight_copies[q].start()
    for d in AHEAD[1:]:
        send_tokens(d)

    loads[2].wait()
    loads[3].wait()
    loads[4].wait()

    def grad_step(i, _):
        at = pl.ds(pl.multiple_of(i * 512, 512), 512)
        grad = lax.dot_general(tf[...], cv[:, at], (((1,), (0,)), ((), ())), preferred_element_type=F32)
        fv[:, at] = (0.9 * mv[:, at].astype(F32) + 0.1 * (grad * INVERSE)).astype(BF16)
        return _

    lax.fori_loop(0, COLS // 512, grad_step, 0)
    y_copies = [
        remote(fv.at[:, pl.ds(pl.multiple_of(((y + d) % NY) * 128, 128), 128)], yin.at[d - 1],
               (ysend, yrecv), d - 1, y_peers[d - 1])
        for d in range(1, NY)
    ]
    stores = [pltpu.make_async_copy(fv, fresh, local.at[5])]
    stores[0].start()

    @pl.when((from_leader != 0) & (from_leader != 4) & (from_leader != 5))
    def _():
        pl.semaphore_wait(inside, 1)

    @pl.when((from_leader >= 1) & (from_leader <= 4))
    def _():
        signal(inside, left)

    @pl.when(from_leader >= 5)
    def _():
        signal(inside, right)

    @pl.when(leads)
    def _():
        pl.semaphore_wait(inside, 2)
        for p in far:
            signal(others, p)

    def leader_tells():
        @pl.when(leads)
        def _():
            pl.semaphore_wait(others, len(far))
            for d in range(1, NX):
                signal(ready, device(y, zh, c, zl, (x + d) % NX))

    def send_votes():
        @pl.when(jnp.logical_not(leads))
        def _():
            pl.semaphore_wait(ready, 1)

        for q in y_copies:
            q.start()

    loads[0].wait()
    loads[1].wait()

    def own_partial(d, q):
        cols = pl.ds(q * QUARTER, QUARTER)
        own[SLOT[d], :, cols] = INVERSE * lax.dot_general(
            tt[:, pl.ds(piece(d), 128)], ww[:, cols], (((0,), (0,)), ((), ())), preferred_element_type=F32
        )

    def own_partials(d):
        token_copies[d].wait_recv()
        for q in range(4):
            own_partial(d, q)

    messages = {}

    def quarter(way, m):
        return ((m // 2 + way) % 2) * 2 + m % 2

    def owner(way, m):
        ahead = 4 - (m // 2 + 1) // 2
        return ahead if way == 0 else (NX - ahead) % NX

    def send_sum(way, m):
        at = way * 14 + m
        total = own[SLOT[owner(way, m)], :, pl.ds(quarter(way, m) * QUARTER, QUARTER)]
        if m >= 4:
            messages[way, m - 4].wait_recv()
            total = total + ring_in[at - 4].astype(F32)
        ring_out[at] = total.astype(BF16)
        messages[way, m] = remote(ring_out.at[at], ring_in.at[at], (xsend, xrecv), at,
                                  right if way == 0 else left)
        messages[way, m].start()

    def send_step(k):
        for m in (2 * k, 2 * k + 1):
            for way in range(2):
                send_sum(way, m)

    def input_grad_part(first, last):
        def step(i, _):
            at = pl.ds(pl.multiple_of(i * 512, 512), 512)
            gv[:, at] = (
                lax.dot_general(ww[pl.ds(0, FEAT)], cv[at, :], (((1,), (1,)), ((), ())),
                                preferred_element_type=F32) * INVERSE
            ).astype(BF16)
            return _

        lax.fori_loop(first, last, step, 0)

    token_copies[4].wait_recv()
    for m in range(2):
        for way in (1, 0):
            q = quarter(way, m)
            weight_copies[q].wait_recv()
            own_partial(4, q)
            send_sum(way, m)
    own_partials(3)
    own_partials(5)
    send_step(1)
    input_grad_part(0, 2)
    send_step(2)
    leader_tells()
    own_partials(2)
    own_partials(6)
    send_step(3)
    send_votes()
    input_grad_part(2, 4)
    stores.append(pltpu.make_async_copy(gv, ig, local.at[6]))
    stores[1].start()
    send_step(4)
    own_partials(1)
    own_partials(7)
    send_step(5)
    own_partials(0)
    send_step(6)

    my_block = pl.ds(pl.multiple_of(y * 128, 128), 128)
    total = clipped(fv[:, my_block])
    for d in range(1, NY):
        y_copies[d - 1].wait_recv()
        total = total + clipped(yin[d - 1])
    zout[...] = total.T
    z_copies = [
        remote(zout.at[pl.ds(pl.multiple_of(((zh + d // 2) % NZ) * 32 + ((c + d) % 2) * 16, 16), 16)],
               zin.at[d - 1], (zsend, zrecv), d - 1, z_peers[d - 1])
        for d in range(1, 2 * NZ)
    ]
    for q in z_copies:
        q.start()

    arrived = {(way, quarter(way, m)): m for way in range(2) for m in range(10, 14)}
    for q in (2, 3, 0, 1):
        cols = pl.ds(q * QUARTER, QUARTER)
        total = own[SLOT[0], :, cols]
        for way in range(2):
            messages[way, arrived[way, q]].wait_recv()
            total = total + ring_in[way * 14 + arrived[way, q]].astype(F32)
        kvv[:, cols] = total.astype(BF16)
    stores.append(pltpu.make_async_copy(kvv, kv, local.at[7]))
    stores[2].start()

    own_columns = pl.ds(pl.multiple_of(zh * 32 + c * 16, 16), 16)
    wt[...] = ww[pl.ds(0, FEAT), my_block].astype(F32).T
    lt[...] = jnp.broadcast_to(thr[pl.ds(y, 1), :].astype(F32), (8, 128)).T
    part = zout[own_columns, :]
    for d in range(1, 2 * NZ):
        z_copies[d - 1].wait_recv()
        part = part + zin[d - 1]
    update = jnp.clip(part / lt[own_columns, 0:1], -1.0, 1.0)
    nv[...] = (wt[own_columns, :] - 0.5 * update).astype(BF16)
    stores.append(pltpu.make_async_copy(nv, new_w, local.at[8]))
    stores[3].start()

    for q in weight_copies + [token_copies[d] for d in AHEAD] + y_copies + z_copies:
        q.wait_send()
    for way in range(2):
        for m in range(14):
            messages[way, m].wait_send()
    for q in stores:
        q.wait()


def write_kernel(*refs):
    ins, outs, held, sems = refs[:4], refs[4:8], refs[8:12], refs[12]
    loads = [pltpu.make_async_copy(a, b, sems.at[i]) for i, (a, b) in enumerate(zip(ins, held))]
    stores = [pltpu.make_async_copy(a, b, sems.at[4 + i]) for i, (a, b) in enumerate(zip(held, outs))]
    for q in loads:
        q.start()
    for i in (3, 0, 2, 1):
        loads[i].wait()
        stores[i].start()
    for q in stores:
        q.wait()


ANY = pl.BlockSpec(memory_space=pl.ANY)
HBM = pl.BlockSpec(memory_space=pltpu.HBM)
VMEM = pl.BlockSpec(memory_space=pltpu.VMEM)
DMA = pltpu.SemaphoreType.DMA


def per_device(tokens, cotangent, weight, momentum, threshold):
    shape = jax.ShapeDtypeStruct
    results = pl.pallas_call(
        main_kernel,
        out_shape=(
            shape((128, COLS), BF16),
            shape((FEAT, ROWS), BF16),
            shape((FEAT, COLS), BF16),
            shape((16, FEAT), BF16),
        ),
        in_specs=[HBM] * 4 + [VMEM],
        out_specs=[ANY] * 4,
        scratch_shapes=[
            pltpu.VMEM((FEAT, ROWS), BF16),
            pltpu.VMEM((2 * FEAT, 1024), BF16),
            pltpu.VMEM((2 * FEAT, COLS), BF16),
            pltpu.VMEM((ROWS, COLS), BF16),
            pltpu.VMEM((FEAT, COLS), BF16),
            pltpu.VMEM((FEAT, COLS), BF16),
            pltpu.VMEM((FEAT, ROWS), BF16),
            pltpu.VMEM((NX, 128, COLS), F32),
            pltpu.VMEM((28, 128, QUARTER), BF16),
            pltpu.VMEM((28, 128, QUARTER), BF16),
            pltpu.VMEM((128, COLS), BF16),
            pltpu.VMEM((NY - 1, FEAT, 128), BF16),
            pltpu.VMEM((128, FEAT), F32),
            pltpu.VMEM((2 * NZ - 1, 16, FEAT), F32),
            pltpu.VMEM((128, FEAT), F32),
            pltpu.VMEM((128, 8), F32),
            pltpu.VMEM((16, FEAT), BF16),
            DMA((9,)),
            DMA((4,)), DMA((4,)),
            DMA((8,)), DMA((8,)),
            DMA((28,)), DMA((28,)),
            DMA((7,)), DMA((7,)),
            DMA((7,)), DMA((7,)),
            pltpu.SemaphoreType.REGULAR,
            pltpu.SemaphoreType.REGULAR,
            pltpu.SemaphoreType.REGULAR,
        ],
        compiler_params=pltpu.CompilerParams(
            collective_id=0, has_side_effects=True, vmem_limit_bytes=61 * 2**20
        ),
        cost_estimate=pl.CostEstimate(flops=2_400_000_000, bytes_accessed=7_000_000, transcendentals=0),
        name="keys_and_votes",
    )(tokens.T, cotangent, weight, momentum[0], threshold.reshape(8, 128))
    kv, ig, fresh, new_weight = pl.pallas_call(
        write_kernel,
        out_shape=tuple(shape(a.shape, a.dtype) for a in results),
        in_specs=[ANY] * 4,
        out_specs=[HBM] * 4,
        scratch_shapes=[pltpu.VMEM(a.shape, a.dtype) for a in results] + [DMA((8,))],
        compiler_params=pltpu.CompilerParams(vmem_limit_bytes=61 * 2**20),
        name="write_results",
    )(*results)
    return kv, ig.T, fresh[None], new_weight.T


def solution(mesh):
    return jax.shard_map(
        per_device,
        mesh=mesh,
        in_specs=(P("dp", "tensor"), P("dp", None), P("tensor", None), P("dp", "tensor", None), P()),
        out_specs=(P(("dp", "tensor"), None), P("dp", "tensor"), P("dp", "tensor", None), P("tensor", "dp")),
        check_vma=False,
    )
```

```python
import jax
import jax.numpy as jnp
from jax import lax
from jax.experimental import pallas as pl
from jax.experimental.pallas import tpu as pltpu
from jax.sharding import PartitionSpec as P

D = 3072
INVERSE = D ** (-0.5)
MESH = pl.DeviceIdType.MESH
F32 = jnp.float32
BF16 = jnp.bfloat16

NX, NY, NZ = 8, 8, 4
LEADER = 2
FEAT, ROWS, COLS = 192, 2048, 1024
HALF, QUARTER = COLS // 2, COLS // 4
AHEAD = (4, 3, 5, 2, 6, 1, 7, 0)
SLOT = {d: s for s, d in enumerate(AHEAD)}


def place():
    dp, tensor = lax.axis_index("dp"), lax.axis_index("tensor")
    return dp // 8, (dp // 2) % 4, dp % 2, tensor // 8, tensor % 8


def device(y, z_hi, core, z_lo, x):
    return (y * 8 + z_hi * 2 + core, z_lo * 8 + x)


def remote(src, dst, sems, i, peer):
    send, recv = sems
    return pltpu.make_async_remote_copy(
        src_ref=src,
        dst_ref=dst,
        send_sem=send.at[i],
        recv_sem=recv.at[i],
        device_id=peer,
        device_id_type=MESH,
    )


def signal(semaphore, peer):
    pl.semaphore_signal(semaphore, inc=1, device_id=peer, device_id_type=MESH)


def clipped(m):
    return jnp.clip(m.astype(F32) * 8.0, -1.0, 1.0)


def main_kernel(
    tok, cot, w, mom, thr,
    kv, ig, fresh, new_w,
    tf, tt, ww, cv, mv, fv, gv, own, ring_out, ring_in, kvv, yin, zout, zin, wt, lt, nv,
    local, wsend, wrecv, tsend, trecv, xsend, xrecv, ysend, yrecv, zsend, zrecv, inside, above, below, ready,
):
    y, zh, c, zl, x = place()
    right = device(y, zh, c, zl, (x + 1) % NX)
    left = device(y, zh, c, zl, (x + NX - 1) % NX)
    pair = device(y, zh, c, 1 - zl, x)
    z = zh * 2 + zl
    outer = device(y, (zh + 3 - 2 * zl) % NZ, c, 1 - zl, x)
    inner = (z > 0) & (z < 7)
    feeds_end = (z == 1) | (z == 6)
    y_peers = [device((y + d) % NY, zh, c, zl, x) for d in range(1, NY)]
    z_peers = [device(y, (zh + d // 2) % NZ, (c + d) % 2, zl, x) for d in range(1, 2 * NZ)]

    barrier = pltpu.get_barrier_semaphore()
    from_leader = (x + NX - LEADER) % NX
    leads = from_leader == 0
    peers = [right, left, pair] + y_peers
    for p in peers:
        signal(barrier, p)

    @pl.when(inner)
    def _():
        signal(barrier, outer)

    rank = zh * 2 + c

    def for_ranks(higher, act):
        for r in range(2 * NZ):
            @pl.when(leads & ((r > rank) if higher else (r < rank)))
            def _(r=r):
                act(device(y, r // 2, r % 2, zl, x))

    for_ranks(True, lambda p: signal(barrier, p))

    mine = pl.multiple_of(zl * 1024, 1024)
    theirs = pl.multiple_of((1 - zl) * 1024, 1024)
    loads = [
        pltpu.make_async_copy(tok.at[:, pl.ds(mine, 1024)], tt.at[pl.ds(0, FEAT)], local.at[0]),
        pltpu.make_async_copy(w, ww.at[pl.ds(0, FEAT)], local.at[1]),
        pltpu.make_async_copy(tok, tf, local.at[2]),
        pltpu.make_async_copy(mom, mv, local.at[3]),
        pltpu.make_async_copy(cot, cv, local.at[4]),
    ]
    for load in loads:
        load.start()

    pl.semaphore_wait(barrier, len(peers) + inner.astype(jnp.int32) + leads.astype(jnp.int32) * rank)

    def piece(d):
        return pl.multiple_of(((x + d) % NX) * 128, 128)

    token_copies = {}

    def send_tokens(d):
        token_copies[d] = remote(
            tok.at[:, pl.ds(pl.multiple_of(theirs + piece(d), 128), 128)],
            tt.at[pl.ds(FEAT, FEAT), pl.ds(piece(d), 128)],
            (tsend, trecv), SLOT[d], pair,
        )
        token_copies[d].start()

    weight_copies = [
        remote(w.at[:, pl.ds(q * QUARTER, QUARTER)], ww.at[pl.ds(FEAT, FEAT), pl.ds(q * QUARTER, QUARTER)],
               (wsend, wrecv), q, pair if q < 2 else outer)
        for q in range(4)
    ]
    end_copies = [
        pltpu.make_async_remote_copy(
            src_ref=w.at[:, pl.ds(q * QUARTER, QUARTER)],
            dst_ref=ww.at[pl.ds(FEAT, FEAT), pl.ds(q * QUARTER, QUARTER)],
            send_sem=wsend.at[q + 2], recv_sem=wrecv.at[q], device_id=pair, device_id_type=MESH,
        )
        for q in (2, 3)
    ]
    send_tokens(4)
    for q in (2, 0, 3, 1):
        if q < 2:
            weight_copies[q].start()
        else:
            pl.when(inner)(weight_copies[q].start)
            pl.when(feeds_end)(end_copies[q - 2].start)
    for d in AHEAD[1:]:
        send_tokens(d)

    loads[2].wait()
    loads[3].wait()
    loads[4].wait()

    def grad_step(i, _):
        at = pl.ds(pl.multiple_of(i * 512, 512), 512)
        grad = lax.dot_general(tf[...], cv[:, at], (((1,), (0,)), ((), ())), preferred_element_type=F32)
        fv[:, at] = (0.9 * mv[:, at].astype(F32) + 0.1 * (grad * INVERSE)).astype(BF16)
        return _

    lax.fori_loop(0, COLS // 512, grad_step, 0)
    y_copies = [
        remote(fv.at[:, pl.ds(pl.multiple_of(((y + d) % NY) * 128, 128), 128)], yin.at[d - 1],
               (ysend, yrecv), d - 1, y_peers[d - 1])
        for d in range(1, NY)
    ]
    for q in y_copies:
        q.start()
    stores = [pltpu.make_async_copy(fv, fresh, local.at[5])]
    stores[0].start()

    @pl.when((from_leader != 0) & (from_leader != 4) & (from_leader != 5))
    def _():
        pl.semaphore_wait(inside, 1)

    @pl.when((from_leader >= 1) & (from_leader <= 4))
    def _():
        signal(inside, left)

    @pl.when(from_leader >= 5)
    def _():
        signal(inside, right)

    @pl.when(leads)
    def _():
        pl.semaphore_wait(inside, 2)

    for_ranks(False, lambda p: signal(above, p))

    def leader_tells():
        @pl.when(leads & (rank < 2 * NZ - 1))
        def _():
            pl.semaphore_wait(above, 2 * NZ - 1 - rank)

        for_ranks(True, lambda p: signal(below, p))

        @pl.when(leads & (rank > 0))
        def _():
            pl.semaphore_wait(below, rank)

        @pl.when(leads)
        def _():
            for d in range(1, NX):
                signal(ready, device(y, zh, c, zl, (x + d) % NX))

    my_block = pl.ds(pl.multiple_of(y * 128, 128), 128)

    def sum_votes():
        total = clipped(fv[:, my_block])
        for d in range(1, NY):
            y_copies[d - 1].wait_recv()
            total = total + clipped(yin[d - 1])
        zout[...] = total.T

    z_copies = [
        remote(zout.at[pl.ds(pl.multiple_of(((zh + d // 2) % NZ) * 32 + ((c + d) % 2) * 16, 16), 16)],
               zin.at[d - 1], (zsend, zrecv), d - 1, z_peers[d - 1])
        for d in range(1, 2 * NZ)
    ]


    def send_votes():
        @pl.when(jnp.logical_not(leads))
        def _():
            pl.semaphore_wait(ready, 1)

        for q in z_copies:
            q.start()

    loads[0].wait()
    loads[1].wait()

    def own_partial(d, q):
        cols = pl.ds(q * QUARTER, QUARTER)
        own[SLOT[d], :, cols] = INVERSE * lax.dot_general(
            tt[:, pl.ds(piece(d), 128)], ww[:, cols], (((0,), (0,)), ((), ())), preferred_element_type=F32
        )

    def own_partials(d):
        token_copies[d].wait_recv()
        for q in range(4):
            own_partial(d, q)

    messages = {}

    def quarter(way, m):
        return ((m // 2 + way) % 2) * 2 + m % 2

    def owner(way, m):
        ahead = 4 - (m // 2 + 1) // 2
        return ahead if way == 0 else (NX - ahead) % NX

    def send_sum(way, m):
        at = way * 14 + m
        total = own[SLOT[owner(way, m)], :, pl.ds(quarter(way, m) * QUARTER, QUARTER)]
        if m >= 4:
            messages[way, m - 4].wait_recv()
            total = total + ring_in[at - 4].astype(F32)
        ring_out[at] = total.astype(BF16)
        messages[way, m] = remote(ring_out.at[at], ring_in.at[at], (xsend, xrecv), at,
                                  right if way == 0 else left)
        messages[way, m].start()

    def send_step(k):
        for m in (2 * k, 2 * k + 1):
            for way in range(2):
                send_sum(way, m)

    def input_grad_part(first, last):
        def step(i, _):
            at = pl.ds(pl.multiple_of(i * 512, 512), 512)
            gv[:, at] = (
                lax.dot_general(ww[pl.ds(0, FEAT)], cv[at, :], (((1,), (1,)), ((), ())),
                                preferred_element_type=F32) * INVERSE
            ).astype(BF16)
            return _

        lax.fori_loop(first, last, step, 0)

    token_copies[4].wait_recv()
    for m in range(2):
        for way in (1, 0):
            q = quarter(way, m)
            weight_copies[q].wait_recv()
            own_partial(4, q)
            send_sum(way, m)
    own_partials(3)
    own_partials(5)
    send_step(1)
    input_grad_part(0, 2)
    send_step(2)
    own_partials(2)
    own_partials(6)
    sum_votes()
    send_step(3)
    leader_tells()
    input_grad_part(2, 4)
    stores.append(pltpu.make_async_copy(gv, ig, local.at[6]))
    stores[1].start()
    send_step(4)
    send_votes()
    own_partials(1)
    own_partials(7)
    send_step(5)
    own_partials(0)
    send_step(6)

    arrived = {(way, quarter(way, m)): m for way in range(2) for m in range(10, 14)}
    for q in (2, 3, 0, 1):
        cols = pl.ds(q * QUARTER, QUARTER)
        total = own[SLOT[0], :, cols]
        for way in range(2):
            messages[way, arrived[way, q]].wait_recv()
            total = total + ring_in[way * 14 + arrived[way, q]].astype(F32)
        kvv[:, cols] = total.astype(BF16)
    stores.append(pltpu.make_async_copy(kvv, kv, local.at[7]))
    stores[2].start()

    own_columns = pl.ds(pl.multiple_of(zh * 32 + c * 16, 16), 16)
    wt[...] = ww[pl.ds(0, FEAT), my_block].astype(F32).T
    lt[...] = jnp.broadcast_to(thr[pl.ds(y, 1), :].astype(F32), (8, 128)).T
    part = zout[own_columns, :]
    for d in range(1, 2 * NZ):
        z_copies[d - 1].wait_recv()
        part = part + zin[d - 1]
    update = jnp.clip(part / lt[own_columns, 0:1], -1.0, 1.0)
    nv[...] = (wt[own_columns, :] - 0.5 * update).astype(BF16)
    stores.append(pltpu.make_async_copy(nv, new_w, local.at[8]))
    stores[3].start()

    for q in weight_copies[2:]:
        pl.when(inner)(q.wait_send)
    for q in end_copies:
        pl.when(feeds_end)(q.wait_send)
    for q in weight_copies[:2] + [token_copies[d] for d in AHEAD] + y_copies + z_copies:
        q.wait_send()
    for way in range(2):
        for m in range(14):
            messages[way, m].wait_send()
    for q in stores:
        q.wait()


def write_kernel(*refs):
    ins, outs, held, sems = refs[:4], refs[4:8], refs[8:12], refs[12]
    loads = [pltpu.make_async_copy(a, b, sems.at[i]) for i, (a, b) in enumerate(zip(ins, held))]
    stores = [pltpu.make_async_copy(a, b, sems.at[4 + i]) for i, (a, b) in enumerate(zip(held, outs))]
    for q in loads:
        q.start()
    for i in (3, 0, 2, 1):
        loads[i].wait()
        stores[i].start()
    for q in stores:
        q.wait()


ANY = pl.BlockSpec(memory_space=pl.ANY)
HBM = pl.BlockSpec(memory_space=pltpu.HBM)
VMEM = pl.BlockSpec(memory_space=pltpu.VMEM)
DMA = pltpu.SemaphoreType.DMA


def per_device(tokens, cotangent, weight, momentum, threshold):
    shape = jax.ShapeDtypeStruct
    results = pl.pallas_call(
        main_kernel,
        out_shape=(
            shape((128, COLS), BF16),
            shape((FEAT, ROWS), BF16),
            shape((FEAT, COLS), BF16),
            shape((16, FEAT), BF16),
        ),
        in_specs=[HBM] * 4 + [VMEM],
        out_specs=[ANY] * 4,
        scratch_shapes=[
            pltpu.VMEM((FEAT, ROWS), BF16),
            pltpu.VMEM((2 * FEAT, 1024), BF16),
            pltpu.VMEM((2 * FEAT, COLS), BF16),
            pltpu.VMEM((ROWS, COLS), BF16),
            pltpu.VMEM((FEAT, COLS), BF16),
            pltpu.VMEM((FEAT, COLS), BF16),
            pltpu.VMEM((FEAT, ROWS), BF16),
            pltpu.VMEM((NX, 128, COLS), F32),
            pltpu.VMEM((28, 128, QUARTER), BF16),
            pltpu.VMEM((28, 128, QUARTER), BF16),
            pltpu.VMEM((128, COLS), BF16),
            pltpu.VMEM((NY - 1, FEAT, 128), BF16),
            pltpu.VMEM((128, FEAT), F32),
            pltpu.VMEM((2 * NZ - 1, 16, FEAT), F32),
            pltpu.VMEM((128, FEAT), F32),
            pltpu.VMEM((128, 8), F32),
            pltpu.VMEM((16, FEAT), BF16),
            DMA((9,)),
            DMA((6,)), DMA((4,)),
            DMA((8,)), DMA((8,)),
            DMA((28,)), DMA((28,)),
            DMA((7,)), DMA((7,)),
            DMA((7,)), DMA((7,)),
            pltpu.SemaphoreType.REGULAR,
            pltpu.SemaphoreType.REGULAR,
            pltpu.SemaphoreType.REGULAR,
            pltpu.SemaphoreType.REGULAR,
        ],
        compiler_params=pltpu.CompilerParams(
            collective_id=0, has_side_effects=True, vmem_limit_bytes=61 * 2**20
        ),
        cost_estimate=pl.CostEstimate(flops=2_400_000_000, bytes_accessed=7_000_000, transcendentals=0),
        name="keys_and_votes",
    )(tokens.T, cotangent, weight, momentum[0], threshold.reshape(8, 128))
    kv, ig, fresh, new_weight = pl.pallas_call(
        write_kernel,
        out_shape=tuple(shape(a.shape, a.dtype) for a in results),
        in_specs=[ANY] * 4,
        out_specs=[HBM] * 4,
        scratch_shapes=[pltpu.VMEM(a.shape, a.dtype) for a in results] + [DMA((8,))],
        compiler_params=pltpu.CompilerParams(vmem_limit_bytes=61 * 2**20),
        name="write_results",
    )(*results)
    return kv, ig.T, fresh[None], new_weight.T


def solution(mesh):
    return jax.shard_map(
        per_device,
        mesh=mesh,
        in_specs=(P("dp", "tensor"), P("dp", None), P("tensor", None), P("dp", "tensor", None), P()),
        out_specs=(P(("dp", "tensor"), None), P("dp", "tensor"), P("dp", "tensor", None), P("tensor", "dp")),
        check_vma=False,
    )
```

```python
import jax
import jax.numpy as jnp
from jax import lax
from jax.experimental import pallas as pl
from jax.experimental.pallas import tpu as pltpu
from jax.sharding import PartitionSpec as P

D = 3072
INVERSE = D ** (-0.5)
MESH = pl.DeviceIdType.MESH
F32 = jnp.float32
BF16 = jnp.bfloat16

NX, NY, NZ = 8, 8, 4
LEADER = 2
FEAT, ROWS, COLS = 192, 2048, 1024
HALF, QUARTER = COLS // 2, COLS // 4
AHEAD = (4, 3, 5, 2, 6, 1, 7, 0)
SLOT = {d: s for s, d in enumerate(AHEAD)}


def place():
    dp, tensor = lax.axis_index("dp"), lax.axis_index("tensor")
    return dp // 8, (dp // 2) % 4, dp % 2, tensor // 8, tensor % 8


def device(y, z_hi, core, z_lo, x):
    return (y * 8 + z_hi * 2 + core, z_lo * 8 + x)


def remote(src, dst, sems, i, peer):
    send, recv = sems
    return pltpu.make_async_remote_copy(
        src_ref=src,
        dst_ref=dst,
        send_sem=send.at[i],
        recv_sem=recv.at[i],
        device_id=peer,
        device_id_type=MESH,
    )


def signal(semaphore, peer):
    pl.semaphore_signal(semaphore, inc=1, device_id=peer, device_id_type=MESH)


def clipped(m):
    return jnp.clip(m.astype(F32) * 8.0, -1.0, 1.0)


def main_kernel(
    tok, cot, w, mom, thr,
    kv, ig, fresh, new_w,
    tf, tt, ww, cv, mv, fv, gv, own, ring_out, ring_in, kvv, yin, zout, zin, wt, lt, nv,
    local, wsend, wrecv, tsend, trecv, xsend, xrecv, ysend, yrecv, zsend, zrecv, inside, above, below, ready,
):
    y, zh, c, zl, x = place()
    right = device(y, zh, c, zl, (x + 1) % NX)
    left = device(y, zh, c, zl, (x + NX - 1) % NX)
    pair = device(y, zh, c, 1 - zl, x)
    z = zh * 2 + zl
    outer = device(y, (zh + 3 - 2 * zl) % NZ, c, 1 - zl, x)
    inner = (z > 0) & (z < 7)
    feeds_end = (z == 1) | (z == 6)
    y_peers = [device((y + d) % NY, zh, c, zl, x) for d in range(1, NY)]
    z_peers = [device(y, (zh + d // 2) % NZ, (c + d) % 2, zl, x) for d in range(1, 2 * NZ)]

    barrier = pltpu.get_barrier_semaphore()
    from_leader = (x + NX - LEADER) % NX
    leads = from_leader == 0
    peers = [right, left, pair] + y_peers
    for p in peers:
        signal(barrier, p)

    @pl.when(inner)
    def _():
        signal(barrier, outer)

    rank = zh * 2 + c

    def for_ranks(higher, act):
        for r in range(2 * NZ):
            @pl.when(leads & ((r > rank) if higher else (r < rank)))
            def _(r=r):
                act(device(y, r // 2, r % 2, zl, x))

    for_ranks(True, lambda p: signal(barrier, p))

    mine = pl.multiple_of(zl * 1024, 1024)
    theirs = pl.multiple_of((1 - zl) * 1024, 1024)
    loads = [
        pltpu.make_async_copy(tok.at[:, pl.ds(mine, 1024)], tt.at[pl.ds(0, FEAT)], local.at[0]),
        pltpu.make_async_copy(w, ww.at[pl.ds(0, FEAT)], local.at[1]),
        pltpu.make_async_copy(tok, tf, local.at[2]),
        pltpu.make_async_copy(mom, mv, local.at[3]),
        pltpu.make_async_copy(cot, cv, local.at[4]),
    ]
    for load in loads:
        load.start()

    pl.semaphore_wait(barrier, len(peers) + inner.astype(jnp.int32) + leads.astype(jnp.int32) * rank)

    def piece(d):
        return pl.multiple_of(((x + d) % NX) * 128, 128)

    token_copies = {}

    def send_tokens(d):
        token_copies[d] = remote(
            tok.at[:, pl.ds(pl.multiple_of(theirs + piece(d), 128), 128)],
            tt.at[pl.ds(FEAT, FEAT), pl.ds(piece(d), 128)],
            (tsend, trecv), SLOT[d], pair,
        )
        token_copies[d].start()

    weight_copies = [
        remote(w.at[:, pl.ds(q * QUARTER, QUARTER)], ww.at[pl.ds(FEAT, FEAT), pl.ds(q * QUARTER, QUARTER)],
               (wsend, wrecv), q, pair if q < 2 else outer)
        for q in range(4)
    ]
    end_copies = [
        pltpu.make_async_remote_copy(
            src_ref=w.at[:, pl.ds(q * QUARTER, QUARTER)],
            dst_ref=ww.at[pl.ds(FEAT, FEAT), pl.ds(q * QUARTER, QUARTER)],
            send_sem=wsend.at[q + 2], recv_sem=wrecv.at[q], device_id=pair, device_id_type=MESH,
        )
        for q in (2, 3)
    ]
    send_tokens(4)
    for q in (2, 0, 3, 1):
        if q < 2:
            weight_copies[q].start()
        else:
            pl.when(inner)(weight_copies[q].start)
            pl.when(feeds_end)(end_copies[q - 2].start)
    for d in AHEAD[1:]:
        send_tokens(d)

    loads[2].wait()
    loads[3].wait()
    loads[4].wait()

    def grad_step(i, _):
        at = pl.ds(pl.multiple_of(i * 512, 512), 512)
        grad = lax.dot_general(tf[...], cv[:, at], (((1,), (0,)), ((), ())), preferred_element_type=F32)
        fv[:, at] = (0.9 * mv[:, at].astype(F32) + 0.1 * (grad * INVERSE)).astype(BF16)
        return _

    lax.fori_loop(0, COLS // 512, grad_step, 0)
    y_copies = [
        remote(fv.at[:, pl.ds(pl.multiple_of(((y + d) % NY) * 128, 128), 128)], yin.at[d - 1],
               (ysend, yrecv), d - 1, y_peers[d - 1])
        for d in range(1, NY)
    ]
    for q in y_copies:
        q.start()
    stores = [pltpu.make_async_copy(fv, fresh, local.at[5])]
    stores[0].start()

    @pl.when((from_leader != 0) & (from_leader != 4) & (from_leader != 5))
    def _():
        pl.semaphore_wait(inside, 1)

    @pl.when((from_leader >= 1) & (from_leader <= 4))
    def _():
        signal(inside, left)

    @pl.when(from_leader >= 5)
    def _():
        signal(inside, right)

    @pl.when(leads)
    def _():
        pl.semaphore_wait(inside, 2)

    for_ranks(False, lambda p: signal(above, p))

    def leader_tells():
        @pl.when(leads & (rank < 2 * NZ - 1))
        def _():
            pl.semaphore_wait(above, 2 * NZ - 1 - rank)

        for_ranks(True, lambda p: signal(below, p))

        @pl.when(leads & (rank > 0))
        def _():
            pl.semaphore_wait(below, rank)

        @pl.when(leads)
        def _():
            for d in range(1, NX):
                signal(ready, device(y, zh, c, zl, (x + d) % NX))

    my_block = pl.ds(pl.multiple_of(y * 128, 128), 128)

    def sum_votes():
        total = clipped(fv[:, my_block])
        for d in range(1, NY):
            y_copies[d - 1].wait_recv()
            total = total + clipped(yin[d - 1])
        zout[...] = total.T

    z_copies = [
        remote(zout.at[pl.ds(pl.multiple_of(((zh + d // 2) % NZ) * 32 + ((c + d) % 2) * 16, 16), 16)],
               zin.at[d - 1], (zsend, zrecv), d - 1, z_peers[d - 1])
        for d in range(1, 2 * NZ)
    ]


    def send_votes():
        @pl.when(jnp.logical_not(leads))
        def _():
            pl.semaphore_wait(ready, 1)

        for q in z_copies:
            q.start()

    loads[0].wait()
    loads[1].wait()

    def own_partial(d, q):
        cols = pl.ds(q * QUARTER, QUARTER)
        own[SLOT[d], :, cols] = INVERSE * lax.dot_general(
            tt[:, pl.ds(piece(d), 128)], ww[:, cols], (((0,), (0,)), ((), ())), preferred_element_type=F32
        )

    def own_partials(d):
        token_copies[d].wait_recv()
        for q in range(4):
            own_partial(d, q)

    messages = {}

    def quarter(way, m):
        return ((m // 2 + way) % 2) * 2 + m % 2

    def owner(way, m):
        ahead = 4 - (m // 2 + 1) // 2
        return ahead if way == 0 else (NX - ahead) % NX

    def send_sum(way, m):
        at = way * 14 + m
        total = own[SLOT[owner(way, m)], :, pl.ds(quarter(way, m) * QUARTER, QUARTER)]
        if m >= 4:
            messages[way, m - 4].wait_recv()
            total = total + ring_in[at - 4].astype(F32)
        ring_out[at] = total.astype(BF16)
        messages[way, m] = remote(ring_out.at[at], ring_in.at[at], (xsend, xrecv), at,
                                  right if way == 0 else left)
        messages[way, m].start()

    def send_step(k):
        for m in (2 * k, 2 * k + 1):
            for way in range(2):
                send_sum(way, m)

    def input_grad_part(first, last):
        def step(i, _):
            at = pl.ds(pl.multiple_of(i * 512, 512), 512)
            gv[:, at] = (
                lax.dot_general(ww[pl.ds(0, FEAT)], cv[at, :], (((1,), (1,)), ((), ())),
                                preferred_element_type=F32) * INVERSE
            ).astype(BF16)
            return _

        lax.fori_loop(first, last, step, 0)

    token_copies[4].wait_recv()
    for m in range(2):
        for way in (1, 0):
            q = quarter(way, m)
            weight_copies[q].wait_recv()
            own_partial(4, q)
            send_sum(way, m)
    own_partials(3)
    own_partials(5)
    send_step(1)
    input_grad_part(0, 2)
    send_step(2)
    own_partials(2)
    own_partials(6)
    sum_votes()
    leader_tells()
    send_step(3)
    send_votes()
    input_grad_part(2, 4)
    stores.append(pltpu.make_async_copy(gv, ig, local.at[6]))
    stores[1].start()
    send_step(4)
    own_partials(1)
    own_partials(7)
    send_step(5)
    own_partials(0)
    send_step(6)

    arrived = {(way, quarter(way, m)): m for way in range(2) for m in range(10, 14)}
    for q in (2, 3, 0, 1):
        cols = pl.ds(q * QUARTER, QUARTER)
        total = own[SLOT[0], :, cols]
        for way in range(2):
            messages[way, arrived[way, q]].wait_recv()
            total = total + ring_in[way * 14 + arrived[way, q]].astype(F32)
        kvv[:, cols] = total.astype(BF16)
    stores.append(pltpu.make_async_copy(kvv, kv, local.at[7]))
    stores[2].start()

    own_columns = pl.ds(pl.multiple_of(zh * 32 + c * 16, 16), 16)
    wt[...] = ww[pl.ds(0, FEAT), my_block].astype(F32).T
    lt[...] = jnp.broadcast_to(thr[pl.ds(y, 1), :].astype(F32), (8, 128)).T
    part = zout[own_columns, :]
    for d in range(1, 2 * NZ):
        z_copies[d - 1].wait_recv()
        part = part + zin[d - 1]
    update = jnp.clip(part / lt[own_columns, 0:1], -1.0, 1.0)
    nv[...] = (wt[own_columns, :] - 0.5 * update).astype(BF16)
    stores.append(pltpu.make_async_copy(nv, new_w, local.at[8]))
    stores[3].start()

    for q in weight_copies[2:]:
        pl.when(inner)(q.wait_send)
    for q in end_copies:
        pl.when(feeds_end)(q.wait_send)
    for q in weight_copies[:2] + [token_copies[d] for d in AHEAD] + y_copies + z_copies:
        q.wait_send()
    for way in range(2):
        for m in range(14):
            messages[way, m].wait_send()
    for q in stores:
        q.wait()


def write_kernel(*refs):
    ins, outs, held, sems = refs[:4], refs[4:8], refs[8:12], refs[12]
    loads = [pltpu.make_async_copy(a, b, sems.at[i]) for i, (a, b) in enumerate(zip(ins, held))]
    stores = [pltpu.make_async_copy(a, b, sems.at[4 + i]) for i, (a, b) in enumerate(zip(held, outs))]
    for q in loads:
        q.start()
    for i in (3, 0, 2, 1):
        loads[i].wait()
        stores[i].start()
    for q in stores:
        q.wait()


ANY = pl.BlockSpec(memory_space=pl.ANY)
HBM = pl.BlockSpec(memory_space=pltpu.HBM)
VMEM = pl.BlockSpec(memory_space=pltpu.VMEM)
DMA = pltpu.SemaphoreType.DMA


def per_device(tokens, cotangent, weight, momentum, threshold):
    shape = jax.ShapeDtypeStruct
    results = pl.pallas_call(
        main_kernel,
        out_shape=(
            shape((128, COLS), BF16),
            shape((FEAT, ROWS), BF16),
            shape((FEAT, COLS), BF16),
            shape((16, FEAT), BF16),
        ),
        in_specs=[HBM] * 4 + [VMEM],
        out_specs=[ANY] * 4,
        scratch_shapes=[
            pltpu.VMEM((FEAT, ROWS), BF16),
            pltpu.VMEM((2 * FEAT, 1024), BF16),
            pltpu.VMEM((2 * FEAT, COLS), BF16),
            pltpu.VMEM((ROWS, COLS), BF16),
            pltpu.VMEM((FEAT, COLS), BF16),
            pltpu.VMEM((FEAT, COLS), BF16),
            pltpu.VMEM((FEAT, ROWS), BF16),
            pltpu.VMEM((NX, 128, COLS), F32),
            pltpu.VMEM((28, 128, QUARTER), BF16),
            pltpu.VMEM((28, 128, QUARTER), BF16),
            pltpu.VMEM((128, COLS), BF16),
            pltpu.VMEM((NY - 1, FEAT, 128), BF16),
            pltpu.VMEM((128, FEAT), F32),
            pltpu.VMEM((2 * NZ - 1, 16, FEAT), F32),
            pltpu.VMEM((128, FEAT), F32),
            pltpu.VMEM((128, 8), F32),
            pltpu.VMEM((16, FEAT), BF16),
            DMA((9,)),
            DMA((6,)), DMA((4,)),
            DMA((8,)), DMA((8,)),
            DMA((28,)), DMA((28,)),
            DMA((7,)), DMA((7,)),
            DMA((7,)), DMA((7,)),
            pltpu.SemaphoreType.REGULAR,
            pltpu.SemaphoreType.REGULAR,
            pltpu.SemaphoreType.REGULAR,
            pltpu.SemaphoreType.REGULAR,
        ],
        compiler_params=pltpu.CompilerParams(
            collective_id=0, has_side_effects=True, vmem_limit_bytes=61 * 2**20
        ),
        cost_estimate=pl.CostEstimate(flops=2_400_000_000, bytes_accessed=7_000_000, transcendentals=0),
        name="keys_and_votes",
    )(tokens.T, cotangent, weight, momentum[0], threshold.reshape(8, 128))
    kv, ig, fresh, new_weight = pl.pallas_call(
        write_kernel,
        out_shape=tuple(shape(a.shape, a.dtype) for a in results),
        in_specs=[ANY] * 4,
        out_specs=[HBM] * 4,
        scratch_shapes=[pltpu.VMEM(a.shape, a.dtype) for a in results] + [DMA((8,))],
        compiler_params=pltpu.CompilerParams(vmem_limit_bytes=61 * 2**20),
        name="write_results",
    )(*results)
    return kv, ig.T, fresh[None], new_weight.T


def solution(mesh):
    return jax.shard_map(
        per_device,
        mesh=mesh,
        in_specs=(P("dp", "tensor"), P("dp", None), P("tensor", None), P("dp", "tensor", None), P()),
        out_specs=(P(("dp", "tensor"), None), P("dp", "tensor"), P("dp", "tensor", None), P("tensor", "dp")),
        check_vma=False,
    )
```
